768 devices in a mesh: col: 96 (over z, y_hi, x), row: 8 (over y_lo, core).
Axes of the slice: x: 4, y: 8 (y_hi: 2, y_lo: 4; y = y_hi * 4 + y_lo), z: 12, core: 2. Of those that a mesh axis runs over, the one named last changes fastest.
Arguments:
- picture_vectors: bfloat16 [147456, 1152], P(('col', 'row')), may hold values from -0.19921875 to 0.19921875
- caption_features: bfloat16 [147456, 1152], P(('col', 'row')), may hold values from -0.19921875 to 0.19921875
- matched_caption_slot: int32 [768, 192], P(('col', 'row')), may hold values from 0 to 191, each once within a row
- caption_mapper_matrix: bfloat16 [1152, 1152], replicated, may hold values from -0.1875 to 0.1875
- mapper_intercept: float32 [1152], replicated, may hold values from -0.2 to 0.2
- sharpness_factor: float32 [1], replicated, may hold values from 2 to 6
- score_shift_vector: float32 [1], replicated, may hold values from -2 to 0
Outputs:
- image_grad: float32 [147456, 1152], P(('col', 'row'))
- text_grad: float32 [147456, 1152], P(('col', 'row'))
- head_grad: float32 [1152, 1152], P('row')
- bias_grad: float32 [1152], P('row')
The draws below stay inside these ranges and needn't reach their ends.
Inputs may be any that keep to these rules, and one draw needn't show every extreme that they name: `matched_caption_slot`: each row of 192 entries holds every number of 0 to 191 once.
All inputs are finite; a program needn't handle non-finite values.
Results may differ from the reference program's by a relative error of at most 0.025.
Values may be sent and summed in bfloat16 or wider, within the bound.
No kernel may reach another device: no remote copies, remote signals or barrier semaphores. Data moves between devices by JAX's collectives and lax.ppermute only.
A program may use at most 64 MiB of HBM per device.

```python
import jax
import jax.numpy as jnp
from jax import lax

D = 1152
IMG_DEV = 192
BLOCKS = 768
IMAGES = 147456
N_COL = 96
N_ROW = 8


def steps_of(key, shape, split, smallest, largest):
    factor_of = 1.0
    for axis_at, parts in split:
        draws = jax.random.uniform(jax.random.fold_in(jax.random.fold_in(key, 6), axis_at), (parts,), jnp.float32, smallest / len(split), largest / len(split))
        factor_of = factor_of * jnp.repeat(jnp.exp(draws), shape[axis_at] // parts).reshape((-1,) + (1,) * (len(shape) - 1 - axis_at))
    return factor_of


def gaussian(rng, shape, width, most, split=(), held_as=jnp.bfloat16):
    values = jax.random.normal(rng, shape, jnp.float32) * width
    if len(split) > 0:
        values = steps_of(rng, shape, split, -0.22, 0.18) * values
    return jnp.clip(values, min=-most, max=most).astype(held_as)


def setup_inputs(seed: int = 0) -> dict:
    key_list = jax.random.split(jax.random.key(seed), 8)
    return {
        "picture_vectors": gaussian(key_list[0], (IMAGES, D), 0.03, 0.19921875, ((0, 768),)),
        "caption_features": gaussian(key_list[1], (IMAGES, D), 0.03, 0.19921875, ((0, 768),)),
        "matched_caption_slot": jax.vmap(lambda own: jax.random.permutation(own, IMG_DEV))(jax.random.split(key_list[2], BLOCKS)).reshape((BLOCKS, IMG_DEV)).astype(jnp.int32),
        "caption_mapper_matrix": gaussian(key_list[3], (D, D), D ** -0.5, 0.1875),
        "mapper_intercept": gaussian(key_list[4], (D,), 0.03, 0.2, (), jnp.float32),
        "sharpness_factor": jnp.clip(jax.random.uniform(key_list[5], (1,), jnp.float32, 2.0, 6.0), 2.0, 6.0),
        "score_shift_vector": jnp.clip(jax.random.uniform(key_list[6], (1,), jnp.float32, -2.0, 0.0), -2.0, 0.0),
    }


eps = 1e-06

def unit_rows(values):
    scale = lax.rsqrt(lax.optimization_barrier(jnp.sum(values * values, -1, keepdims=True)) + eps)
    return (values * scale, scale)

def unit_back(grad, unit, scale):
    return (grad - unit * lax.optimization_barrier(jnp.sum(unit * grad, -1, keepdims=True))) * scale

def reference(picture_vectors, caption_features, matched_caption_slot, caption_mapper_matrix, mapper_intercept, sharpness_factor, score_shift_vector):
    score_sharpness = sharpness_factor[0]
    cyclic_displacement = score_shift_vector[0]
    group_rows = N_ROW * IMG_DEV
    image_groups = picture_vectors.reshape(N_COL, group_rows, D)
    text_groups = jnp.roll(caption_features.reshape(N_COL, group_rows, D), 1, axis=0)
    pair_groups = matched_caption_slot.reshape(N_COL, N_ROW, IMG_DEV)

    def group(carry, inputs):
        image_rows, text_rows, perm = inputs
        projected = jnp.dot(text_rows, caption_mapper_matrix, preferred_element_type=jnp.float32) + mapper_intercept
        text_unit_embedding, text_scale = unit_rows(projected)
        image_unit, image_scale = unit_rows(image_rows.astype(jnp.float32))
        caption_reduced = text_unit_embedding.astype(jnp.bfloat16)
        picture_reduced = image_unit.astype(jnp.bfloat16)
        similarity_grid = score_sharpness * jnp.dot(picture_reduced, caption_reduced.T, preferred_element_type=jnp.float32) + cyclic_displacement
        target = (jnp.arange(N_ROW, dtype=jnp.int32)[:, None] * IMG_DEV + perm).reshape(-1)
        positive = target[:, None] == jnp.arange(group_rows, dtype=jnp.int32)[None, :]
        sign = jnp.where(positive, 1.0, -1.0).astype(jnp.float32)
        coefficient_entry = (-sign * jax.nn.sigmoid(-sign * similarity_grid)).astype(jnp.bfloat16)
        picture_direction = score_sharpness * jnp.dot(coefficient_entry, caption_reduced, preferred_element_type=jnp.float32)
        coefficient_tiles = coefficient_entry.astype(jnp.float32).reshape(N_ROW, IMG_DEV, group_rows)
        picture_tiles = picture_reduced.astype(jnp.float32).reshape(N_ROW, IMG_DEV, D)
        portions = (score_sharpness * jnp.einsum('qzf,qzo->qfo', coefficient_tiles, picture_tiles)).astype(jnp.bfloat16)
        portions = lax.optimization_barrier(portions).astype(jnp.float32)
        text_dir = lax.optimization_barrier(jnp.sum(portions, 0))
        image_grad = unit_back(picture_direction, image_unit, image_scale)
        projected_text_gradient = unit_back(text_dir, text_unit_embedding, text_scale).astype(jnp.bfloat16)
        text_grad = jnp.dot(projected_text_gradient, caption_mapper_matrix.T, preferred_element_type=jnp.float32)
        text_blocks = text_rows.astype(jnp.float32).reshape(N_ROW, IMG_DEV, D)
        grad_blocks = projected_text_gradient.astype(jnp.float32).reshape(N_ROW, IMG_DEV, D)
        head_parts = jnp.einsum('rid,rie->rde', text_blocks, grad_blocks).astype(jnp.bfloat16)
        head_parts = lax.optimization_barrier(head_parts).astype(jnp.float32)
        bias_parts = lax.optimization_barrier(jnp.sum(grad_blocks, 1)).astype(jnp.bfloat16)
        bias_parts = lax.optimization_barrier(bias_parts).astype(jnp.float32)
        carry = (carry[0] + lax.optimization_barrier(jnp.sum(head_parts, 0)), carry[1] + lax.optimization_barrier(jnp.sum(bias_parts, 0)))
        return (carry, (image_grad, text_grad))
    init = (jnp.zeros((D, D), jnp.float32), jnp.zeros((D,), jnp.float32))
    sums, grads = lax.scan(group, init, (image_groups, text_groups, pair_groups))
    image_grad = grads[0].reshape(N_COL * group_rows, D)
    text_grad = grads[1].reshape(N_COL * group_rows, D)
    return (image_grad, text_grad, sums[0], sums[1])
```

```python
import jax
import jax.numpy as jnp
from jax import lax
from jax.sharding import PartitionSpec as P

eps = 1e-06
AXES = ("z", "h", "x", "y", "k")
COL = AXES[:3]
SIZES = (12, 2, 4, 4, 2)
D = 1152
PART = 36
PAD = 40
f32, bf16 = jnp.float32, jnp.bfloat16


def swap(block, axis, mask):
    n = lax.axis_size(axis)
    return lax.ppermute(block, axis, [(i, i ^ mask) for i in range(n)])


def turn(block, axis, distance):
    n = lax.axis_size(axis)
    return lax.ppermute(block, axis, [(i, (i + distance) % n) for i in range(n)])


def low(values):
    return lax.reduce_precision(values, 8, 7).astype(bf16)


def dot(a, b, ca, cb):
    return lax.dot_general(a, b, (((ca,), (cb,)), ((), ())), preferred_element_type=f32)


def halve(both, bit, axis, mask):
    sent = lax.dynamic_index_in_dim(both, 1 - bit, 0, keepdims=False)
    kept = lax.dynamic_index_in_dim(both, bit, 0, keepdims=False)
    return low(kept.astype(f32) + swap(sent, axis, mask).astype(f32))


def join(own, bit, axis, mask):
    other = swap(own, axis, mask)
    first = jnp.where(bit == 0, own, other)
    second = jnp.where(bit == 0, other, own)
    return jnp.stack([first, second])


def spread_matrix():
    place = jnp.arange(32 * PAD, dtype=jnp.int32)
    part, i = place // PAD, place % PAD
    k, q, b, a = part // 16, part // 4 % 4, part // 2 % 2, part % 2
    feature = jnp.where(i < PART, ((2 * a + b) * 2 + k) * 144 + q * PART + i, -1)
    matrix = (jnp.arange(D, dtype=jnp.int32)[:, None] == feature[None, :]).astype(bf16)
    return matrix, (i == PART).astype(f32)


def per_device(pictures, captions, slot, matrix, intercept, sharpness, score_shift):
    sharp, moved = sharpness[0], score_shift[0]
    rows = pictures.shape[0]
    z, x, y, k = (lax.axis_index(a) for a in ("z", "x", "y", "k"))

    paired = turn_col(captions)
    picture = pictures.astype(f32)
    image_scale = lax.rsqrt(jnp.sum(picture * picture, -1, keepdims=True) + eps)
    image_unit = picture * image_scale
    image_low = image_unit.astype(bf16)
    pair = jnp.concatenate([image_low, swap(image_low, "y", 2)])
    images = jnp.concatenate([pair, swap(pair, "k", 1)])
    texts = jnp.concatenate([paired, swap(paired, "y", 1)])

    projected = dot(texts, matrix, 1, 0) + intercept
    text_scale = lax.rsqrt(jnp.sum(projected * projected, -1, keepdims=True) + eps)
    text_unit = projected * text_scale
    text_low = text_unit.astype(bf16)
    spread, ones = spread_matrix()
    texts_spread = (dot(texts, spread, 1, 0) + ones).astype(bf16)

    scores = sharp * dot(images, text_low, 1, 1) + moved
    wanted = jnp.concatenate([slot[0], jnp.full((3 * rows,), -1, jnp.int32)])
    positive = wanted[:, None] == jnp.arange(2 * rows, dtype=jnp.int32)[None, :]
    sign = jnp.where(positive, 1.0, -1.0).astype(f32)
    weight = (-sign * jax.nn.sigmoid(-sign * scores)).astype(bf16)

    text_dir = sharp * dot(weight, images, 0, 0)
    along = jnp.sum(text_unit * text_dir, -1, keepdims=True)
    grad = (text_dir - text_unit * along) * text_scale
    grad_low = low(grad)

    head = dot(texts_spread, grad_low, 0, 0).astype(bf16).reshape(2, 2, 2, 2, 2, PAD, D)
    head = halve(head, k, "k", 1)
    head = halve(head, (x // 2) ^ (x % 2), "x", 1)
    head = halve(head, x // 2, "x", 3)
    head = halve(head, y % 2, "y", 1)
    head = halve(head, y // 2, "y", 2)
    head = low(head.astype(f32) + swap(head, "h", 1).astype(f32))
    head = low(head.astype(f32) + swap(head, "z", 1).astype(f32))
    head = low(head.astype(f32) + swap(head, "z", 2).astype(f32))
    ring = [head, turn(head, "z", 8), turn(head, "z", 4)]
    u = z // 4
    total = 0.0
    for j in range(3):
        at = (j - u) % 3
        total = total + jnp.where(at == 0, ring[0], jnp.where(at == 1, ring[1], ring[2])).astype(f32)
    head = low(total)
    head = join(head, x // 2, "x", 3)
    head = join(head, (x // 2) ^ (x % 2), "x", 1).reshape(4, PAD, D)
    head_grad = head[:, :PART].reshape(4 * PART, D).astype(f32)
    bias_grad = lax.dynamic_slice(head[0, PART].astype(f32), ((2 * y + k) * 144,), (144,))

    projected_grad = grad_low[:rows].astype(f32) + swap(grad_low[rows:], "y", 1).astype(f32)
    text_grad = dot(projected_grad.astype(bf16), matrix, 1, 1)

    image_dir = sharp * dot(weight, text_low, 1, 0)
    mine = image_dir[: 2 * rows] + swap(image_dir[2 * rows :].astype(bf16), "k", 1).astype(f32)
    own = mine[:rows] + swap(mine[rows:].astype(bf16), "y", 2).astype(f32)
    along = jnp.sum(image_unit * own, -1, keepdims=True)
    image_grad = (own - image_unit * along) * image_scale
    return (image_grad, text_grad, head_grad, bias_grad)


def turn_col(block):
    return lax.ppermute(block, COL, [((i - 1) % 96, i) for i in range(96)])


def solution(mesh):
    fine = jax.sharding.Mesh(mesh.devices.reshape(SIZES), AXES)
    rows = P(AXES, None)
    in_specs = (rows, rows, rows, P(), P(), P(), P())
    out_specs = (rows, rows, P(("y", "k"), None), P(("y", "k")))
    return jax.shard_map(
        per_device, mesh=fine, in_specs=in_specs, out_specs=out_specs, check_vma=False
    )
```

```python
import jax
import jax.numpy as jnp
from jax import lax
from jax.sharding import PartitionSpec as P

eps = 1e-06
AXES = ("z", "h", "x", "y", "k")
COL = AXES[:3]
SIZES = (12, 2, 4, 4, 2)
D = 1152
PART = 36
PAD = 40
f32, bf16 = jnp.float32, jnp.bfloat16


def swap(block, axis, mask):
    n = lax.axis_size(axis)
    return lax.ppermute(block, axis, [(i, i ^ mask) for i in range(n)])


def turn(block, axis, distance):
    n = lax.axis_size(axis)
    return lax.ppermute(block, axis, [(i, (i + distance) % n) for i in range(n)])


def low(values):
    return lax.reduce_precision(values, 8, 7).astype(bf16)


def dot(a, b, ca, cb):
    return lax.dot_general(a, b, (((ca,), (cb,)), ((), ())), preferred_element_type=f32)


def pick(parts, at):
    total = 0.0
    for part in parts:
        total = total + lax.dynamic_index_in_dim(part, at, 0, keepdims=False).astype(f32)
    return total


def tie(*values):
    return lax.optimization_barrier(values)


def spread_matrix(core):
    place = jnp.arange(16 * PAD, dtype=jnp.int32)
    part, i = place // PAD, place % PAD
    x, y = part // 4, part % 4
    feature = jnp.where(i < PART, (2 * y + core) * 144 + x * PART + i, -1)
    matrix = (jnp.arange(D, dtype=jnp.int32)[:, None] == feature[None, :]).astype(bf16)
    return matrix, (i == PART).astype(f32)


def head_rows(texts, core):
    spread, ones = spread_matrix(core)
    (spread,) = tie(spread)
    return (dot(texts, spread, 1, 0) + ones).astype(bf16)


def per_device(pictures, captions, slot, matrix, intercept, sharpness, score_shift):
    sharp, moved = sharpness[0], score_shift[0]
    rows = pictures.shape[0]
    z, x, y, k = (lax.axis_index(a) for a in ("z", "x", "y", "k"))

    paired = turn_col(captions)
    picture = pictures.astype(f32)
    image_scale = lax.rsqrt(jnp.sum(picture * picture, -1, keepdims=True) + eps)
    image_unit = picture * image_scale
    image_low = image_unit.astype(bf16)
    pair = jnp.concatenate([image_low, swap(image_low, "y", 2)])
    images = jnp.concatenate([pair, swap(pair, "k", 1)])
    texts = jnp.concatenate([paired, swap(paired, "y", 1)])

    projected = dot(texts, matrix, 1, 0) + intercept
    text_scale = lax.rsqrt(jnp.sum(projected * projected, -1, keepdims=True) + eps)
    text_unit = projected * text_scale
    text_low = text_unit.astype(bf16)
    texts_sent, texts_kept = tie(head_rows(texts, 1 - k), head_rows(texts, k))

    scores = sharp * dot(images, text_low, 1, 1) + moved
    wanted = jnp.concatenate([slot[0], jnp.full((3 * rows,), -1, jnp.int32)])
    positive = wanted[:, None] == jnp.arange(2 * rows, dtype=jnp.int32)[None, :]
    sign = jnp.where(positive, 1.0, -1.0).astype(f32)
    weight = (-sign * jax.nn.sigmoid(-sign * scores)).astype(bf16)

    text_dir = sharp * dot(weight, images, 0, 0)
    along = jnp.sum(text_unit * text_dir, -1, keepdims=True)
    grad = (text_dir - text_unit * along) * text_scale
    grad_low = low(grad)

    sent = dot(texts_sent, grad_low, 0, 0).astype(bf16)
    arrived = swap(sent, "k", 1)
    kept = dot(texts_kept, grad_low, 0, 0).astype(bf16)
    parts = [p.reshape(4, 4 * PAD, D) for p in (kept, arrived)]

    over_x = {d: turn(low(pick(parts, (x + d) % 4)), "x", d) for d in (2, 1, 3)}
    grad_far = swap(grad_low[rows:], "y", 1)
    image_dir = sharp * dot(weight, text_low, 1, 0)
    image_sent = image_dir[2 * rows :].astype(bf16)
    *over_x, image_sent, grad_far = tie(*over_x.values(), image_sent, grad_far)
    projected_grad = grad_low[:rows].astype(f32) + grad_far.astype(f32)
    text_grad = dot(projected_grad.astype(bf16), matrix, 1, 1)

    parts = [lax.dynamic_index_in_dim(p, x, 0, keepdims=False) for p in parts] + over_x
    parts = [p.reshape(4, PAD, D) for p in parts]
    over_y = {m: swap(low(pick(parts, y ^ m)), "y", m) for m in (2, 3, 1)}
    total = pick(parts, y)
    for other in over_y.values():
        total = total + other.astype(f32)
    head = low(total)
    head = low(head.astype(f32) + swap(head, "h", 1).astype(f32))

    mine = image_dir[: 2 * rows] + swap(image_sent, "k", 1).astype(f32)
    image_far = mine[rows:].astype(bf16)
    head, image_far = tie(head, image_far)

    over_z = {m: swap(head, "z", m).astype(f32) for m in (2, 3, 1)}
    head = low((head.astype(f32) + over_z[1]) + (over_z[2] + over_z[3]))
    far_one = swap(image_far[: rows // 2], "y", 2)
    head, far_one = tie(head, far_one)
    ring = [head, turn(head, "z", 8), turn(head, "z", 4)]
    u = z // 4
    total = 0.0
    for j in range(3):
        at = (j - u) % 3
        total = total + jnp.where(at == 0, ring[0], jnp.where(at == 1, ring[1], ring[2])).astype(f32)
    far_two = swap(image_far[rows // 2 :], "y", 2)
    head, far_two = tie(low(total), far_two)
    own = mine[:rows] + jnp.concatenate([far_one, far_two]).astype(f32)
    around = [head] + [turn(head, "x", d) for d in (2, 1, 3)]
    ordered = []
    for q in range(4):
        d = (x - q) % 4
        one = jnp.where(d == 0, around[0], jnp.where(d == 2, around[1], jnp.where(d == 1, around[2], around[3])))
        ordered.append(one)
    head_grad = jnp.concatenate([one[:PART] for one in ordered]).astype(f32)
    bias_grad = lax.dynamic_slice(ordered[0][PART].astype(f32), ((2 * y + k) * 144,), (144,))

    along = jnp.sum(image_unit * own, -1, keepdims=True)
    image_grad = (own - image_unit * along) * image_scale
    return (image_grad, text_grad, head_grad, bias_grad)


def turn_col(block):
    return lax.ppermute(block, COL, [((i - 1) % 96, i) for i in range(96)])


def solution(mesh):
    fine = jax.sharding.Mesh(mesh.devices.reshape(SIZES), AXES)
    rows = P(AXES, None)
    in_specs = (rows, rows, rows, P(), P(), P(), P())
    out_specs = (rows, rows, P(("y", "k"), None), P(("y", "k")))
    return jax.shard_map(
        per_device, mesh=fine, in_specs=in_specs, out_specs=out_specs, check_vma=False
    )
```

```python
import jax
import jax.numpy as jnp
from jax import lax
from jax.sharding import PartitionSpec as P

eps = 1e-06
AXES = ("z", "h", "x", "y", "k")
COL = AXES[:3]
SIZES = (12, 2, 4, 4, 2)
D = 1152
PART = 36
PAD = 40
f32, bf16 = jnp.float32, jnp.bfloat16


def swap(block, axis, mask):
    n = lax.axis_size(axis)
    return lax.ppermute(block, axis, [(i, i ^ mask) for i in range(n)])


def turn(block, axis, distance):
    n = lax.axis_size(axis)
    return lax.ppermute(block, axis, [(i, (i + distance) % n) for i in range(n)])


def low(values):
    return lax.reduce_precision(values, 8, 7).astype(bf16)


def dot(a, b, ca, cb):
    return lax.dot_general(a, b, (((ca,), (cb,)), ((), ())), preferred_element_type=f32)


def pick(parts, at):
    total = 0.0
    for part in parts:
        total = total + lax.dynamic_index_in_dim(part, at, 0, keepdims=False).astype(f32)
    return total


def tie(*values):
    return lax.optimization_barrier(values)


def spread_matrix(core):
    place = jnp.arange(16 * PAD, dtype=jnp.int32)
    part, i = place // PAD, place % PAD
    x, y = part // 4, part % 4
    feature = jnp.where(i < PART, (2 * y + core) * 144 + x * PART + i, -1)
    matrix = (jnp.arange(D, dtype=jnp.int32)[:, None] == feature[None, :]).astype(bf16)
    return matrix, (i == PART).astype(f32)


def head_rows(texts, core):
    spread, ones = spread_matrix(core)
    (spread,) = tie(spread)
    return (dot(texts, spread, 1, 0) + ones).astype(bf16)


def per_device(pictures, captions, slot, matrix, intercept, sharpness, score_shift):
    sharp, moved = sharpness[0], score_shift[0]
    rows = pictures.shape[0]
    z, x, y, k = (lax.axis_index(a) for a in ("z", "x", "y", "k"))

    paired, crossed = shifted(captions, x)
    picture = pictures.astype(f32)
    image_scale = lax.rsqrt(jnp.sum(picture * picture, -1, keepdims=True) + eps)
    image_unit = picture * image_scale
    image_low = image_unit.astype(bf16)
    image_core = swap(image_low, "k", 1)
    image_out, _ = tie(image_low, crossed)
    image_far = swap(image_out, "y", 2)
    images = jnp.concatenate([image_low, image_far, image_core, swap(image_far, "k", 1)])
    texts = jnp.concatenate([paired, swap(paired, "y", 1)])

    projected = dot(texts, matrix, 1, 0) + intercept
    text_scale = lax.rsqrt(jnp.sum(projected * projected, -1, keepdims=True) + eps)
    text_unit = projected * text_scale
    text_low = text_unit.astype(bf16)
    (texts_sent,) = tie(head_rows(texts, 1 - k))

    scores = sharp * dot(images, text_low, 1, 1) + moved
    wanted = jnp.concatenate([slot[0], jnp.full((3 * rows,), -1, jnp.int32)])
    positive = wanted[:, None] == jnp.arange(2 * rows, dtype=jnp.int32)[None, :]
    sign = jnp.where(positive, 1.0, -1.0).astype(f32)
    weight = (-sign * jax.nn.sigmoid(-sign * scores)).astype(bf16)

    text_dir = sharp * dot(weight, images, 0, 0)
    along = jnp.sum(text_unit * text_dir, -1, keepdims=True)
    grad = (text_dir - text_unit * along) * text_scale
    grad_low = low(grad)

    sent = dot(texts_sent, grad_low, 0, 0).astype(bf16)
    sent, texts = tie(sent, texts)
    arrived = swap(sent, "k", 1)
    kept = dot(head_rows(texts, k), grad_low, 0, 0).astype(bf16)
    parts = [p.reshape(4, 4 * PAD, D) for p in (kept, arrived)]

    pieces = [low(pick(parts, (x + d) % 4)) for d in (2, 1, 3)]
    *pieces, weight, grad_sent = tie(*pieces, weight, grad_low[rows:])
    over_x = [turn(piece, "x", d) for piece, d in zip(pieces, (2, 1, 3))]
    image_sent = (sharp * dot(weight[2 * rows :], text_low, 1, 0)).astype(bf16)
    image_core = swap(image_sent, "k", 1)
    grad_far = swap(grad_sent, "y", 1)
    image_kept = sharp * dot(weight[: 2 * rows], text_low, 1, 0)
    image_sent = low(image_kept[rows:] + image_core[rows:].astype(f32))
    far_one = swap(image_sent[: rows // 2], "y", 2)
    *over_x, image_sent, grad_far, far_one = tie(*over_x, image_sent, grad_far, far_one)
    far_two = swap(image_sent[rows // 2 :], "y", 2)
    projected_grad = grad_low[:rows].astype(f32) + grad_far.astype(f32)
    text_grad = dot(projected_grad.astype(bf16), matrix, 1, 1)

    parts = [lax.dynamic_index_in_dim(p, x, 0, keepdims=False) for p in parts] + over_x
    parts = [p.reshape(4, PAD, D) for p in parts]
    over_y = {m: swap(low(pick(parts, y ^ m)), "y", m) for m in (2, 3, 1)}
    total = pick(parts, y)
    for other in over_y.values():
        total = total + other.astype(f32)
    head = low(total)
    head = low(head.astype(f32) + swap(head, "h", 1).astype(f32))

    head, far_two = tie(head, far_two)
    own = image_kept[:rows] + image_core[:rows].astype(f32)
    own = own + jnp.concatenate([far_one, far_two]).astype(f32)

    over_z = {m: swap(head, "z", m).astype(f32) for m in (2, 3, 1)}
    head = low((head.astype(f32) + over_z[1]) + (over_z[2] + over_z[3]))
    ring = [head, turn(head, "z", 8), turn(head, "z", 4)]
    u = z // 4
    total = 0.0
    for j in range(3):
        at = (j - u) % 3
        total = total + jnp.where(at == 0, ring[0], jnp.where(at == 1, ring[1], ring[2])).astype(f32)
    head = low(total)
    around = [head] + [turn(head, "x", d) for d in (2, 1, 3)]
    ordered = []
    for q in range(4):
        d = (x - q) % 4
        one = jnp.where(d == 0, around[0], jnp.where(d == 2, around[1], jnp.where(d == 1, around[2], around[3])))
        ordered.append(one)
    head_grad = jnp.concatenate([one[:PART] for one in ordered]).astype(f32)
    bias_grad = lax.dynamic_slice(ordered[0][PART].astype(f32), ((2 * y + k) * 144,), (144,))

    along = jnp.sum(image_unit * own, -1, keepdims=True)
    image_grad = (own - image_unit * along) * image_scale
    return (image_grad, text_grad, head_grad, bias_grad)


def shifted(block, x):
    def cross(half, plane):
        pairs = []
        for group in range(plane, 96, 4):
            pairs.append((group, (group + 4) % 96))
        return lax.ppermute(half, COL, pairs)

    half = block.shape[0] // 2
    low_half, high_half = tie(block[:half], block[half:])
    crossed = cross(high_half, 3)
    moved = turn(low_half, "x", 1)
    first = jnp.where(x == 0, cross(moved, 0), moved)
    second = turn(jnp.where(x == 3, crossed, high_half), "x", 1)
    return jnp.concatenate([first, second]), crossed


def solution(mesh):
    fine = jax.sharding.Mesh(mesh.devices.reshape(SIZES), AXES)
    rows = P(AXES, None)
    in_specs = (rows, rows, rows, P(), P(), P(), P())
    out_specs = (rows, rows, P(("y", "k"), None), P(("y", "k")))
    return jax.shard_map(
        per_device, mesh=fine, in_specs=in_specs, out_specs=out_specs, check_vma=False
    )
```

```python
import jax
import jax.numpy as jnp
from jax import lax
from jax.sharding import PartitionSpec as P

eps = 1e-06
AXES = ("z", "h", "x", "y", "k")
COL = AXES[:3]
SIZES = (12, 2, 4, 4, 2)
D = 1152
PART = 36
PAD = 40
f32, bf16 = jnp.float32, jnp.bfloat16


def swap(block, axis, mask):
    n = lax.axis_size(axis)
    return lax.ppermute(block, axis, [(i, i ^ mask) for i in range(n)])


def turn(block, axis, distance):
    n = lax.axis_size(axis)
    return lax.ppermute(block, axis, [(i, (i + distance) % n) for i in range(n)])


def low(values):
    return lax.reduce_precision(values, 8, 7).astype(bf16)


def dot(a, b, ca, cb):
    return lax.dot_general(a, b, (((ca,), (cb,)), ((), ())), preferred_element_type=f32)


def pick(parts, at):
    total = 0.0
    for part in parts:
        total = total + lax.dynamic_index_in_dim(part, at, 0, keepdims=False).astype(f32)
    return total


def tie(*values):
    return lax.optimization_barrier(values)


def spread_matrix(core):
    place = jnp.arange(16 * PAD, dtype=jnp.int32)
    part, i = place // PAD, place % PAD
    x, y = part // 4, part % 4
    feature = jnp.where(i < PART, (2 * y + core) * 144 + x * PART + i, -1)
    matrix = (jnp.arange(D, dtype=jnp.int32)[:, None] == feature[None, :]).astype(bf16)
    return matrix, (i == PART).astype(f32)


def head_rows(texts, core):
    spread, ones = spread_matrix(core)
    (spread,) = tie(spread)
    return (dot(texts, spread, 1, 0) + ones).astype(bf16)


def per_device(pictures, captions, slot, matrix, intercept, sharpness, score_shift):
    sharp, moved = sharpness[0], score_shift[0]
    rows = pictures.shape[0]
    z, x, y, k = (lax.axis_index(a) for a in ("z", "x", "y", "k"))

    paired, moved_half = shifted(captions, x)
    picture = pictures.astype(f32)
    image_scale = lax.rsqrt(jnp.sum(picture * picture, -1, keepdims=True) + eps)
    image_unit = picture * image_scale
    image_low = image_unit.astype(bf16)
    image_out, _ = tie(image_low, moved_half)
    image_far = swap(image_out, "y", 2)
    image_core = swap(image_out, "k", 1)
    images = jnp.concatenate([image_low, image_far, image_core, swap(image_far, "k", 1)])
    texts = jnp.concatenate([paired, swap(paired, "y", 1)])

    projected = dot(texts, matrix, 1, 0) + intercept
    text_scale = lax.rsqrt(jnp.sum(projected * projected, -1, keepdims=True) + eps)
    text_unit = projected * text_scale
    text_low = text_unit.astype(bf16)
    texts_sent, texts_kept = tie(head_rows(texts, 1 - k), head_rows(texts, k))

    scores = sharp * dot(images, text_low, 1, 1) + moved
    wanted = jnp.concatenate([slot[0], jnp.full((3 * rows,), -1, jnp.int32)])
    positive = wanted[:, None] == jnp.arange(2 * rows, dtype=jnp.int32)[None, :]
    sign = jnp.where(positive, 1.0, -1.0).astype(f32)
    weight = (-sign * jax.nn.sigmoid(-sign * scores)).astype(bf16)

    text_dir = sharp * dot(weight, images, 0, 0)
    along = jnp.sum(text_unit * text_dir, -1, keepdims=True)
    grad = (text_dir - text_unit * along) * text_scale
    grad_low = low(grad)

    sent = dot(texts_sent, grad_low, 0, 0).astype(bf16)
    arrived = swap(sent, "k", 1)
    kept = dot(texts_kept, grad_low, 0, 0).astype(bf16)
    parts = [p.reshape(4, 4 * PAD, D) for p in (kept, arrived)]

    over_x = [turn(low(pick(parts, (x + d) % 4)), "x", d) for d in (2, 1, 3)]
    grad_far = swap(grad_low[rows:], "y", 1)
    image_sent = (sharp * dot(weight[2 * rows :], text_low, 1, 0)).astype(bf16)
    image_kept = sharp * dot(weight[: 2 * rows], text_low, 1, 0)
    *over_x, image_sent, grad_far = tie(*over_x, image_sent, grad_far)
    image_core = swap(image_sent, "k", 1)
    projected_grad = grad_low[:rows].astype(f32) + grad_far.astype(f32)
    text_grad = dot(projected_grad.astype(bf16), matrix, 1, 1)

    parts = [lax.dynamic_index_in_dim(p, x, 0, keepdims=False) for p in parts] + over_x
    parts = [p.reshape(4, PAD, D) for p in parts]
    over_y = {m: swap(low(pick(parts, y ^ m)), "y", m) for m in (2, 3, 1)}
    *over_y, image_core = tie(*over_y.values(), image_core)
    total = pick(parts, y)
    for other in over_y:
        total = total + other.astype(f32)
    head = low(total)
    head = low(head.astype(f32) + swap(head, "h", 1).astype(f32))

    image_out = (image_kept[rows:] + image_core[rows:].astype(f32)).astype(bf16)
    head, image_out = tie(head, image_out)
    third = rows // 3
    far = [swap(image_out[i * third : (i + 1) * third], "y", 2) for i in range(3)]
    over_z = [swap(head, "z", m) for m in (2, 3, 1)]
    *over_z, far[0] = tie(*over_z, far[0])
    over_z = [other.astype(f32) for other in over_z]
    head = low((head.astype(f32) + over_z[2]) + (over_z[0] + over_z[1]))
    over_z = [turn(head, "z", 8), turn(head, "z", 4)]
    *over_z, far[1] = tie(*over_z, far[1])
    ring = [head] + over_z
    u = z // 4
    total = 0.0
    for j in range(3):
        at = (j - u) % 3
        total = total + jnp.where(at == 0, ring[0], jnp.where(at == 1, ring[1], ring[2])).astype(f32)
    head = low(total)
    around = [head] + [turn(head, "x", d) for d in (2, 1, 3)]
    ordered = []
    for q in range(4):
        d = (x - q) % 4
        one = jnp.where(d == 0, around[0], jnp.where(d == 2, around[1], jnp.where(d == 1, around[2], around[3])))
        ordered.append(one)
    head_grad = jnp.concatenate([one[:PART] for one in ordered]).astype(f32)
    bias_grad = lax.dynamic_slice(ordered[0][PART].astype(f32), ((2 * y + k) * 144,), (144,))

    own = image_kept[:rows] + image_core[:rows].astype(f32) + jnp.concatenate(far).astype(f32)
    along = jnp.sum(image_unit * own, -1, keepdims=True)
    image_grad = (own - image_unit * along) * image_scale
    return (image_grad, text_grad, head_grad, bias_grad)


def shifted(block, x):
    def cross(half, plane):
        pairs = []
        for group in range(plane, 96, 4):
            pairs.append((group, (group + 4) % 96))
        return lax.ppermute(half, COL, pairs)

    half = block.shape[0] // 2
    low_half, high_half = tie(block[:half], block[half:])
    crossed = cross(high_half, 3)
    moved = turn(low_half, "x", 1)
    first = jnp.where(x == 0, cross(moved, 0), moved)
    second = turn(jnp.where(x == 3, crossed, high_half), "x", 1)
    return jnp.concatenate([first, second]), moved


def solution(mesh):
    fine = jax.sharding.Mesh(mesh.devices.reshape(SIZES), AXES)
    rows = P(AXES, None)
    in_specs = (rows, rows, rows, P(), P(), P(), P())
    out_specs = (rows, rows, P(("y", "k"), None), P(("y", "k")))
    return jax.shard_map(
        per_device, mesh=fine, in_specs=in_specs, out_specs=out_specs, check_vma=False
    )
```

```python
import jax
import jax.numpy as jnp
from jax import lax
from jax.sharding import PartitionSpec as P

eps = 1e-06
AXES = ("z", "h", "x", "y", "k")
COL = AXES[:3]
SIZES = (12, 2, 4, 4, 2)
D = 1152
PART = 36
PAD = 40
f32, bf16 = jnp.float32, jnp.bfloat16


def swap(block, axis, mask):
    n = lax.axis_size(axis)
    return lax.ppermute(block, axis, [(i, i ^ mask) for i in range(n)])


def turn(block, axis, distance):
    n = lax.axis_size(axis)
    return lax.ppermute(block, axis, [(i, (i + distance) % n) for i in range(n)])


def low(values):
    return lax.reduce_precision(values, 8, 7).astype(bf16)


def dot(a, b, ca, cb):
    return lax.dot_general(a, b, (((ca,), (cb,)), ((), ())), preferred_element_type=f32)


def pick(parts, at):
    total = 0.0
    for part in parts:
        total = total + lax.dynamic_index_in_dim(part, at, 0, keepdims=False).astype(f32)
    return total


def tie(*values):
    return lax.optimization_barrier(values)


def spread_matrix(core):
    place = jnp.arange(16 * PAD, dtype=jnp.int32)
    part, i = place // PAD, place % PAD
    x, y = part // 4, part % 4
    feature = jnp.where(i < PART, (2 * y + core) * 144 + x * PART + i, -1)
    matrix = (jnp.arange(D, dtype=jnp.int32)[:, None] == feature[None, :]).astype(bf16)
    return matrix, (i == PART).astype(f32)


def head_rows(texts, core):
    spread, ones = spread_matrix(core)
    (spread,) = tie(spread)
    return (dot(texts, spread, 1, 0) + ones).astype(bf16)


def per_device(pictures, captions, slot, matrix, intercept, sharpness, score_shift):
    sharp, moved = sharpness[0], score_shift[0]
    rows = pictures.shape[0]
    z, x, y, k = (lax.axis_index(a) for a in ("z", "x", "y", "k"))

    paired = shifted(captions, x)
    image_far = swap(pictures, "y", 2)
    image_core = swap(pictures, "k", 1)
    texts = jnp.concatenate([paired, swap(paired, "y", 1)])
    texts, image_both = tie(texts, swap(image_far, "k", 1))
    raw = jnp.concatenate([pictures, image_far, image_core, image_both])
    raw = raw.astype(f32)
    image_scale = lax.rsqrt(jnp.sum(raw * raw, -1, keepdims=True) + eps)
    images = (raw * image_scale).astype(bf16)
    image_scale = image_scale[:rows]
    image_unit = pictures.astype(f32) * image_scale

    projected = dot(texts, matrix, 1, 0) + intercept
    text_scale = lax.rsqrt(jnp.sum(projected * projected, -1, keepdims=True) + eps)
    text_unit = projected * text_scale
    text_low = text_unit.astype(bf16)
    texts_sent, texts_kept = tie(head_rows(texts, 1 - k), head_rows(texts, k))

    scores = sharp * dot(images, text_low, 1, 1) + moved
    wanted = jnp.concatenate([slot[0], jnp.full((3 * rows,), -1, jnp.int32)])
    positive = wanted[:, None] == jnp.arange(2 * rows, dtype=jnp.int32)[None, :]
    sign = jnp.where(positive, 1.0, -1.0).astype(f32)
    weight = (-sign * jax.nn.sigmoid(-sign * scores)).astype(bf16)

    text_dir = sharp * dot(weight, images, 0, 0)
    along = jnp.sum(text_unit * text_dir, -1, keepdims=True)
    grad = (text_dir - text_unit * along) * text_scale
    grad_low = low(grad)

    sent = dot(texts_sent, grad_low, 0, 0).astype(bf16)
    arrived = swap(sent, "k", 1)
    kept = dot(texts_kept, grad_low, 0, 0).astype(bf16)
    parts = [p.reshape(4, 4 * PAD, D) for p in (kept, arrived)]

    over_x = [turn(low(pick(parts, (x + d) % 4)), "x", d) for d in (2, 1, 3)]
    grad_far = swap(grad_low[rows:], "y", 1)
    image_sent = (sharp * dot(weight[2 * rows :], text_low, 1, 0)).astype(bf16)
    image_kept = sharp * dot(weight[: 2 * rows], text_low, 1, 0)
    *over_x, image_sent, grad_far = tie(*over_x, image_sent, grad_far)
    image_core = swap(image_sent, "k", 1)
    projected_grad = grad_low[:rows].astype(f32) + grad_far.astype(f32)
    text_grad = dot(projected_grad.astype(bf16), matrix, 1, 1)

    parts = [lax.dynamic_index_in_dim(p, x, 0, keepdims=False) for p in parts] + over_x
    parts = [p.reshape(4, PAD, D) for p in parts]
    over_y = {m: swap(low(pick(parts, y ^ m)), "y", m) for m in (2, 3, 1)}
    *over_y, image_core = tie(*over_y.values(), image_core)
    total = pick(parts, y)
    for other in over_y:
        total = total + other.astype(f32)
    head = low(total)
    head = low(head.astype(f32) + swap(head, "h", 1).astype(f32))

    image_out = (image_kept[rows:] + image_core[rows:].astype(f32)).astype(bf16)
    head, image_out = tie(head, image_out)
    third = rows // 3
    far = [swap(image_out[i * third : (i + 1) * third], "y", 2) for i in range(3)]
    over_z = [swap(head, "z", m) for m in (2, 3, 1)]
    *over_z, far[0] = tie(*over_z, far[0])
    over_z = [other.astype(f32) for other in over_z]
    head = low((head.astype(f32) + over_z[2]) + (over_z[0] + over_z[1]))
    over_z = [turn(head, "z", 8), turn(head, "z", 4)]
    *over_z, far[1] = tie(*over_z, far[1])
    ring = [head] + over_z
    u = z // 4
    total = 0.0
    for j in range(3):
        at = (j - u) % 3
        total = total + jnp.where(at == 0, ring[0], jnp.where(at == 1, ring[1], ring[2])).astype(f32)
    head = low(total)
    around = [head] + [turn(head, "x", d) for d in (2, 1, 3)]
    ordered = []
    for q in range(4):
        d = (x - q) % 4
        one = jnp.where(d == 0, around[0], jnp.where(d == 2, around[1], jnp.where(d == 1, around[2], around[3])))
        ordered.append(one)
    head_grad = jnp.concatenate([one[:PART] for one in ordered]).astype(f32)
    bias_grad = lax.dynamic_slice(ordered[0][PART].astype(f32), ((2 * y + k) * 144,), (144,))

    own = image_kept[:rows] + image_core[:rows].astype(f32) + jnp.concatenate(far).astype(f32)
    along = jnp.sum(image_unit * own, -1, keepdims=True)
    image_grad = (own - image_unit * along) * image_scale
    return (image_grad, text_grad, head_grad, bias_grad)


def shifted(block, x):
    def cross(half, plane):
        pairs = []
        for group in range(plane, 96, 4):
            pairs.append((group, (group + 4) % 96))
        return lax.ppermute(half, COL, pairs)

    half = block.shape[0] // 2
    low_half, high_half = tie(block[:half], block[half:])
    crossed = cross(high_half, 3)
    moved = turn(low_half, "x", 1)
    first = jnp.where(x == 0, cross(moved, 0), moved)
    second = turn(jnp.where(x == 3, crossed, high_half), "x", 1)
    return jnp.concatenate([first, second])


def solution(mesh):
    fine = jax.sharding.Mesh(mesh.devices.reshape(SIZES), AXES)
    rows = P(AXES, None)
    in_specs = (rows, rows, rows, P(), P(), P(), P())
    out_specs = (rows, rows, P(("y", "k"), None), P(("y", "k")))
    return jax.shard_map(
        per_device, mesh=fine, in_specs=in_specs, out_specs=out_specs, check_vma=False
    )
```

```python
import jax
import jax.numpy as jnp
from jax import lax
from jax.sharding import PartitionSpec as P

eps = 1e-06
AXES = ("z", "h", "x", "y", "k")
COL = AXES[:3]
SIZES = (12, 2, 4, 4, 2)
D = 1152
PART = 36
PAD = 40
f32, bf16 = jnp.float32, jnp.bfloat16


def swap(block, axis, mask):
    n = lax.axis_size(axis)
    return lax.ppermute(block, axis, [(i, i ^ mask) for i in range(n)])


def turn(block, axis, distance):
    n = lax.axis_size(axis)
    return lax.ppermute(block, axis, [(i, (i + distance) % n) for i in range(n)])


def low(values):
    return lax.reduce_precision(values, 8, 7).astype(bf16)


def dot(a, b, ca, cb):
    return lax.dot_general(a, b, (((ca,), (cb,)), ((), ())), preferred_element_type=f32)


def pick(parts, at):
    total = 0.0
    for part in parts:
        total = total + lax.dynamic_index_in_dim(part, at, 0, keepdims=False).astype(f32)
    return total


def tie(*values):
    return lax.optimization_barrier(values)


def spread_matrix(core):
    place = jnp.arange(16 * PAD, dtype=jnp.int32)
    part, i = place // PAD, place % PAD
    x, y = part // 4, part % 4
    feature = jnp.where(i < PART, (2 * y + core) * 144 + x * PART + i, -1)
    matrix = (jnp.arange(D, dtype=jnp.int32)[:, None] == feature[None, :]).astype(bf16)
    return matrix, (i == PART).astype(f32)


def head_rows(texts, core):
    spread, ones = spread_matrix(core)
    (spread,) = tie(spread)
    return (dot(texts, spread, 1, 0) + ones).astype(bf16)


def per_device(pictures, captions, slot, matrix, intercept, sharpness, score_shift):
    sharp, moved = sharpness[0], score_shift[0]
    rows = pictures.shape[0]
    z, x, y, k = (lax.axis_index(a) for a in ("z", "x", "y", "k"))

    paired = turn_col(captions)
    picture = pictures.astype(f32)
    image_scale = lax.rsqrt(jnp.sum(picture * picture, -1, keepdims=True) + eps)
    image_unit = picture * image_scale
    image_low = image_unit.astype(bf16)
    pair = jnp.concatenate([image_low, swap(image_low, "y", 2)])
    images = jnp.concatenate([pair, swap(pair, "k", 1)])
    texts = jnp.concatenate([paired, swap(paired, "y", 1)])

    projected = dot(texts, matrix, 1, 0) + intercept
    text_scale = lax.rsqrt(jnp.sum(projected * projected, -1, keepdims=True) + eps)
    text_unit = projected * text_scale
    text_low = text_unit.astype(bf16)
    texts_sent, texts_kept = tie(head_rows(texts, 1 - k), head_rows(texts, k))

    scores = sharp * dot(images, text_low, 1, 1) + moved
    wanted = jnp.concatenate([slot[0], jnp.full((3 * rows,), -1, jnp.int32)])
    positive = wanted[:, None] == jnp.arange(2 * rows, dtype=jnp.int32)[None, :]
    sign = jnp.where(positive, 1.0, -1.0).astype(f32)
    weight = (-sign * jax.nn.sigmoid(-sign * scores)).astype(bf16)

    text_dir = sharp * dot(weight, images, 0, 0)
    along = jnp.sum(text_unit * text_dir, -1, keepdims=True)
    grad = (text_dir - text_unit * along) * text_scale
    grad_low = low(grad)

    sent = dot(texts_sent, grad_low, 0, 0).astype(bf16)
    arrived = swap(sent, "k", 1)
    kept = dot(texts_kept, grad_low, 0, 0).astype(bf16)
    parts = [p.reshape(4, 4 * PAD, D) for p in (kept, arrived)]

    over_x = [turn(low(pick(parts, (x + d) % 4)), "x", d) for d in (2, 1, 3)]
    grad_far = swap(grad_low[rows:], "y", 1)
    image_sent = (sharp * dot(weight[2 * rows :], text_low, 1, 0)).astype(bf16)
    image_kept = sharp * dot(weight[: 2 * rows], text_low, 1, 0)
    *over_x, image_sent, grad_far = tie(*over_x, image_sent, grad_far)
    image_core = swap(image_sent, "k", 1)
    projected_grad = grad_low[:rows].astype(f32) + grad_far.astype(f32)
    text_grad = dot(projected_grad.astype(bf16), matrix, 1, 1)

    parts = [lax.dynamic_index_in_dim(p, x, 0, keepdims=False) for p in parts] + over_x
    parts = [p.reshape(4, PAD, D) for p in parts]
    over_y = {m: swap(low(pick(parts, y ^ m)), "y", m) for m in (2, 3, 1)}
    over_y = list(over_y.values())
    total = pick(parts, y)
    for other in over_y:
        total = total + other.astype(f32)
    head = low(total)
    head = low(head.astype(f32) + swap(head, "h", 1).astype(f32))

    image_out = (image_kept[rows:] + image_core[rows:].astype(f32)).astype(bf16)
    head, image_out = tie(head, image_out)
    far = [swap(image_out[: rows // 2], "y", 2)]
    over_z = [swap(head, "z", m) for m in (2, 3, 1)]
    *over_z, far[0] = tie(*over_z, far[0])
    over_z = [other.astype(f32) for other in over_z]
    head = low((head.astype(f32) + over_z[2]) + (over_z[0] + over_z[1]))
    head, image_late = tie(head, image_out[rows // 2 :])
    far.append(swap(image_late, "y", 2))
    over_z = [turn(head, "z", 8), turn(head, "z", 4)]
    *over_z, far[1] = tie(*over_z, far[1])
    ring = [head] + over_z
    u = z // 4
    total = 0.0
    for j in range(3):
        at = (j - u) % 3
        total = total + jnp.where(at == 0, ring[0], jnp.where(at == 1, ring[1], ring[2])).astype(f32)
    head = low(total)
    around = [head] + [turn(head, "x", d) for d in (2, 1, 3)]
    ordered = []
    for q in range(4):
        d = (x - q) % 4
        one = jnp.where(d == 0, around[0], jnp.where(d == 2, around[1], jnp.where(d == 1, around[2], around[3])))
        ordered.append(one)
    head_grad = jnp.concatenate([one[:PART] for one in ordered]).astype(f32)
    bias_grad = lax.dynamic_slice(ordered[0][PART].astype(f32), ((2 * y + k) * 144,), (144,))

    own = image_kept[:rows] + image_core[:rows].astype(f32) + jnp.concatenate(far).astype(f32)
    along = jnp.sum(image_unit * own, -1, keepdims=True)
    image_grad = (own - image_unit * along) * image_scale
    return (image_grad, text_grad, head_grad, bias_grad)


def turn_col(block):
    return lax.ppermute(block, COL, [((i - 1) % 96, i) for i in range(96)])


def solution(mesh):
    fine = jax.sharding.Mesh(mesh.devices.reshape(SIZES), AXES)
    rows = P(AXES, None)
    in_specs = (rows, rows, rows, P(), P(), P(), P())
    out_specs = (rows, rows, P(("y", "k"), None), P(("y", "k")))
    return jax.shard_map(
        per_device, mesh=fine, in_specs=in_specs, out_specs=out_specs, check_vma=False
    )
```
